512 devices in a mesh: tm: 32 (over y_lo, z), space: 16 (over y_hi, x, core).
Axes of the slice: x: 4, y: 4 (y_hi: 2, y_lo: 2; y = y_hi * 2 + y_lo), z: 16, core: 2. Of those that a mesh axis runs over, the one named last changes fastest.
Arguments:
- cstates: float32 [32, 256, 2048], P('tm', 'space'), may hold values from -4 to 4
- drift: float32 [2, 256, 2048], P(None, 'space'), may hold values from -0.2 to 0.2
- diffusivity: float32 [256, 2048], P('space'), may hold values from 0.1 to 0.24
- coarse_rate: float32 [256, 2048], P('space'), may hold values from 0.00625 to 0.625
Outputs:
- cpoints: float32 [32, 256, 2048], P('tm', 'space')
- coarse_residual: float32 [32, 256, 2048], P('tm', 'space')
The draws below stay inside these ranges and needn't reach their ends.
All inputs are finite; a program needn't handle non-finite values.
Results may differ from the reference program's by a relative error of at most 0.00018.
Values sent between devices are 32-bit elements; how exact they have to be, the bound alone decides.
No kernel may reach another device: no remote copies, remote signals or barrier semaphores. Data moves between devices by JAX's collectives and lax.ppermute only.
A program may use at most 64 MiB of HBM per device.

```python
import math
import jax
import jax.numpy as jnp
from jax import lax

NX = 2048
M = 8
COARSE = 32
NY = 256


def block_levels(stream_key, extent, cuts, least, high):
    def one(dim, blocks):
        draws = jax.random.uniform(jax.random.fold_in(jax.random.fold_in(stream_key, 6), dim), (blocks,), jnp.float32, least / len(cuts), high / len(cuts))
        return jnp.repeat(jnp.exp(draws), extent[dim] // blocks).reshape((-1,) + (1,) * (len(extent) - dim - 1))

    loudness = one(*cuts[0])
    for cut in cuts[1:]:
        loudness = loudness * one(*cut)
    return loudness


def gaussian(rng, shape, scale, limit, pieces=(), dtype=jnp.bfloat16):
    level = block_levels(rng, shape, pieces, -0.22, 0.18) if pieces else 1.0
    values = jax.random.normal(rng, shape, jnp.float32) * scale * level
    return jnp.minimum(jnp.maximum(values, -limit), limit).astype(dtype)


def setup_inputs(seed: int = 0) -> dict:
    streams_of = jax.random.split(jax.random.key(seed), 5)
    cstates = gaussian(streams_of[0], (COARSE, NY, NX), 1.0, 4.0, ((0, 32), (1, 16)), jnp.float32)
    drift = jnp.clip(jax.random.uniform(streams_of[1], (2, NY, NX), jnp.float32, -0.2, 0.2) * block_levels(streams_of[1], (2, NY, NX), ((1, 16),), -0.4, 0.0), -0.2, 0.2)
    diffusivity = jnp.clip(0.1 + 0.13999999 * jax.random.uniform(streams_of[2], (NY, NX), jnp.float32) ** block_levels(streams_of[2], (NY, NX), ((0, 16),), -0.2, 0.2), 0.1, 0.24)
    coarse_rate = jnp.clip(jnp.exp(math.log(0.625) - 4.6051702 * jax.random.uniform(streams_of[3], (NY, NX), jnp.float32) ** block_levels(streams_of[3], (NY, NX), ((0, 16),), -0.2, 0.2)), 0.00625, 0.625)
    return dict(cstates=cstates, drift=drift, diffusivity=diffusivity, coarse_rate=coarse_rate)


nonlinear_weight = 0.05


def advance(field, drift, diffusivity):
    above = jnp.roll(field, -1, axis=-2)
    below = jnp.roll(field, 1, axis=-2)
    right_cell = jnp.roll(field, -1, axis=-1)
    left_cell = jnp.roll(field, 1, axis=-1)
    laplacian = above + below + right_cell + left_cell - 4.0 * field
    transport = (drift[0] + nonlinear_weight * field) * (right_cell - left_cell) * 0.5 + drift[1] * (above - below) * 0.5
    return field + diffusivity * laplacian - transport


def propagate(field, drift, diffusivity):
    for count in range(M):
        field = advance(field, drift, diffusivity)
    return field


def reference(cstates, drift, diffusivity, coarse_rate):
    first = propagate(cstates, drift, diffusivity)
    relaxed = jnp.roll(first, 1, axis=0)
    second = propagate(relaxed, drift, diffusivity)
    coarse_residual = jnp.roll(second, 1, axis=0) - relaxed
    decay = jnp.exp(-coarse_rate)

    def accumulate(carry, term):
        following = decay * carry + term
        return following, following

    closing, unused = lax.scan(accumulate, jnp.zeros_like(decay), coarse_residual)
    last_error = closing / (1.0 - decay ** COARSE)
    unused_last, errors = lax.scan(accumulate, last_error, coarse_residual)
    cpoints = relaxed + errors
    return cpoints, coarse_residual
```

```python
import jax
import jax.numpy as jnp
from jax import lax
from jax.experimental import pallas as pl
from jax.experimental.pallas import tpu as pltpu
from jax.sharding import PartitionSpec as P

M = 8
nonlinear_weight = 0.05


def load_interleaved(dst, source, first, blocks):
    for c in range(source.shape[0]):
        for i in range(blocks):
            dst[c, i] = source[c, pl.ds(first + i, 8, stride=blocks), :]


def steps(state, other, coefs, blocks):
    tiles = state.shape[0]
    lane = lax.broadcasted_iota(jnp.int32, (8, 128), 1)
    is_last, is_first = lane == 127, lane == 0

    def one(src, dst):
        for i in range(blocks):
            to_left = lambda c: pltpu.roll(src[c % tiles, i], 127, 1)
            to_right = lambda c: pltpu.roll(src[c % tiles, i], 1, 1)
            ahead, behind, here = to_left(0), to_right(-1), to_right(0)
            for c in range(tiles):
                u = src[c, i]
                above = src[c, i + 1] if i + 1 < blocks else pltpu.roll(src[c, 0], 7, 0)
                below = src[c, i - 1] if i > 0 else pltpu.roll(src[c, blocks - 1], 1, 0)
                following = to_left(c + 1)
                right = jnp.where(is_last, following, ahead)
                left = jnp.where(is_first, behind, here)
                ahead, behind, here = following, here, to_right(c + 1)
                spread = coefs[2, c, i] * ((above + below) + (right + left))
                along = (coefs[0, c, i] + (0.5 * nonlinear_weight) * u) * (right - left)
                across = coefs[1, c, i] * (above - below)
                dst[c, i] = ((coefs[3, c, i] * u + spread) - along) - across

    def pair(_, carry):
        one(state, other)
        one(other, state)
        return carry

    lax.fori_loop(0, M // 2, pair, 0)


def propagate_kernel(
    cells, drift, diffusivity, rate, before, after, second_out, first_out, term_out, rows, coef_rows, state, other, coefs
):
    height, width = cells.shape
    tiles = width // 128
    for c in range(tiles):
        cols = slice(c * 128, c * 128 + 128)
        rows[c, 0:height] = before[0:height, cols]
        rows[c, height : 2 * height] = cells[:, cols]
        rows[c, 2 * height :] = after[0:height, cols]
        for k in range(3):
            scale = 0.5 if k < 2 else 1.0
            own = drift[k, :, cols] if k < 2 else diffusivity[:, cols]
            part = slice((k + 1) * height, (k + 2) * height)
            coef_rows[k, c, 0:height] = scale * before[part, cols]
            coef_rows[k, c, height : 2 * height] = scale * own
            coef_rows[k, c, 2 * height :] = scale * after[part, cols]

    def phase(first, blocks, out):
        load_interleaved(state, rows, first, blocks)
        for k in range(3):
            load_interleaved(coefs.at[k], coef_rows.at[k], first, blocks)
        for c in range(tiles):
            for i in range(blocks):
                coefs[3, c, i] = 1.0 - 4.0 * coefs[2, c, i]
        steps(state, other, coefs, blocks)
        for c in range(tiles):
            for i in range(blocks):
                rows[c, pl.ds(first + i, 8, stride=blocks), :] = state[c, i]
        for c in range(tiles):
            out[:, c * 128 : c * 128 + 128] = rows[c, height : 2 * height]

    phase(0, 6, first_out)
    phase(8, 4, second_out)
    for r in range(height // 8):
        for c in range(tiles):
            part = (slice(r * 8, r * 8 + 8), slice(c * 128, c * 128 + 128))
            term_out[r * tiles + c] = second_out[part] - jnp.exp(-rate[part]) * first_out[part]


def propagate(cells, drift, diffusivity, rate, before, after):
    height, width = cells.shape
    tiles = height // 8 * (width // 128)
    shape = lambda *s: jax.ShapeDtypeStruct(s, jnp.float32)
    return pl.pallas_call(
        propagate_kernel,
        out_shape=(shape(height, width), shape(height, width), shape(tiles, 8, 128)),
        scratch_shapes=[
            pltpu.VMEM((width // 128, 3 * height, 128), jnp.float32),
            pltpu.VMEM((3, width // 128, 3 * height, 128), jnp.float32),
            pltpu.VMEM((width // 128, 6, 8, 128), jnp.float32),
            pltpu.VMEM((width // 128, 6, 8, 128), jnp.float32),
            pltpu.VMEM((4, width // 128, 6, 8, 128), jnp.float32),
        ],
        compiler_params=pltpu.CompilerParams(vmem_limit_bytes=32 * 1024 * 1024),
        name="propagate",
    )(cells, drift, diffusivity, rate, before, after)


def solve_kernel(terms, rate, points):
    intervals = terms.shape[0]
    decay = jnp.exp(-rate[...])
    power = decay
    for _ in range(intervals.bit_length() - 1):
        power = power * power
    closing = terms[0]
    for j in range(1, intervals):
        closing = decay * closing + terms[j]
    value = closing / (1.0 - power)
    for j in range(intervals):
        value = decay * value + terms[j]
        points[(j + 2) % intervals] = value


def coarse_solve(terms, rate):
    return pl.pallas_call(
        solve_kernel,
        out_shape=jax.ShapeDtypeStruct(terms.shape, jnp.float32),
        name="coarse_solve",
    )(terms, rate)


def passed_along(value, axis, steps):
    count = lax.axis_size(axis)
    return lax.ppermute(value, axis, [(i, (i + steps) % count) for i in range(count)])


def to_tiles(value):
    height, width = value.shape
    return value.reshape(height // 8, 8, width // 128, 128).transpose(0, 2, 1, 3).reshape(-1, 8, 128)


def from_tiles(value, height, width):
    return value.reshape(height // 8, width // 128, 8, 128).transpose(0, 2, 1, 3).reshape(height, width)


def shards(cstates, drift, diffusivity, coarse_rate):
    cells = cstates[0]
    height, width = cells.shape
    message = jnp.concatenate([cells, drift[0], drift[1], diffusivity], axis=0)
    before = passed_along(message, "space", 1)
    after = passed_along(message, "space", -1)
    second, first, term = propagate(cells, drift, diffusivity, coarse_rate, before, after)
    rate = lax.dynamic_index_in_dim(to_tiles(coarse_rate), lax.axis_index("tm"), 0, keepdims=False)
    second_two_on = passed_along(second, "tm", 2)
    first_one_on = passed_along(first, "tm", 1)
    terms = lax.all_to_all(term, "tm", 0, 0, tiled=True)
    points = coarse_solve(terms, rate)
    points = lax.all_to_all(points, "tm", 0, 0, tiled=True)
    cpoints = from_tiles(points, height, width)
    residual = second_two_on - first_one_on
    return cpoints[None], residual[None]


def solution(mesh):
    placed = (P("tm", "space", None), P(None, "space", None), P("space", None), P("space", None))
    return jax.shard_map(
        shards,
        mesh=mesh,
        in_specs=placed,
        out_specs=(P("tm", "space", None), P("tm", "space", None)),
        check_vma=False,
    )
```

```python
import jax
import jax.numpy as jnp
from jax import lax
from jax.experimental import pallas as pl
from jax.experimental.pallas import tpu as pltpu
from jax.sharding import PartitionSpec as P

M = 8
nonlinear_weight = 0.05


def load_interleaved(dst, source, first, blocks):
    for c in range(source.shape[0]):
        for i in range(blocks):
            dst[c, i] = source[c, pl.ds(first + i, 8, stride=blocks), :]


def steps(state, other, coefs, blocks):
    tiles = state.shape[0]
    lane = lax.broadcasted_iota(jnp.int32, (8, 128), 1)
    is_last, is_first = lane == 127, lane == 0

    def one(src, dst):
        for i in range(blocks):
            to_left = lambda c: pltpu.roll(src[c % tiles, i], 127, 1)
            to_right = lambda c: pltpu.roll(src[c % tiles, i], 1, 1)
            ahead, behind, here = to_left(0), to_right(-1), to_right(0)
            for c in range(tiles):
                u = src[c, i]
                above = src[c, i + 1] if i + 1 < blocks else pltpu.roll(src[c, 0], 7, 0)
                below = src[c, i - 1] if i > 0 else pltpu.roll(src[c, blocks - 1], 1, 0)
                following = to_left(c + 1)
                right = jnp.where(is_last, following, ahead)
                left = jnp.where(is_first, behind, here)
                ahead, behind, here = following, here, to_right(c + 1)
                spread = coefs[2, c, i] * ((above + below) + (right + left))
                along = (coefs[0, c, i] + (0.5 * nonlinear_weight) * u) * (right - left)
                across = coefs[1, c, i] * (above - below)
                dst[c, i] = ((coefs[3, c, i] * u + spread) - along) - across

    def pair(_, carry):
        one(state, other)
        one(other, state)
        return carry

    lax.fori_loop(0, M // 2, pair, 0)


def propagate_kernel(
    parity, cells, drift, diffusivity, rate, inner, outer, second_out, first_out, term_out, rows, coef_rows, state, other, coefs
):
    height, width = cells.shape
    tiles = width // 128
    def gather(before, after):
        for c in range(tiles):
            cols = slice(c * 128, c * 128 + 128)
            rows[c, 0:height] = before[0:height, cols]
            rows[c, height : 2 * height] = cells[:, cols]
            rows[c, 2 * height :] = after[0:height, cols]
            for k in range(3):
                scale = 0.5 if k < 2 else 1.0
                own = drift[k, :, cols] if k < 2 else diffusivity[:, cols]
                part = slice((k + 1) * height, (k + 2) * height)
                coef_rows[k, c, 0:height] = scale * before[part, cols]
                coef_rows[k, c, height : 2 * height] = scale * own
                coef_rows[k, c, 2 * height :] = scale * after[part, cols]

    @pl.when(parity[0] == 0)
    def _():
        gather(outer, inner)

    @pl.when(parity[0] == 1)
    def _():
        gather(inner, outer)

    def phase(first, blocks, out):
        load_interleaved(state, rows, first, blocks)
        for k in range(3):
            load_interleaved(coefs.at[k], coef_rows.at[k], first, blocks)
        for c in range(tiles):
            for i in range(blocks):
                coefs[3, c, i] = 1.0 - 4.0 * coefs[2, c, i]
        steps(state, other, coefs, blocks)
        for c in range(tiles):
            for i in range(blocks):
                rows[c, pl.ds(first + i, 8, stride=blocks), :] = state[c, i]
        for c in range(tiles):
            out[:, c * 128 : c * 128 + 128] = rows[c, height : 2 * height]

    phase(0, 6, first_out)
    phase(8, 4, second_out)
    for r in range(height // 8):
        for c in range(tiles):
            part = (slice(r * 8, r * 8 + 8), slice(c * 128, c * 128 + 128))
            term_out[r * tiles + c] = second_out[part] - jnp.exp(-rate[part]) * first_out[part]


def propagate(parity, cells, drift, diffusivity, rate, inner, outer):
    height, width = cells.shape
    tiles = height // 8 * (width // 128)
    shape = lambda *s: jax.ShapeDtypeStruct(s, jnp.float32)
    return pl.pallas_call(
        propagate_kernel,
        out_shape=(shape(height, width), shape(height, width), shape(tiles, 8, 128)),
        scratch_shapes=[
            pltpu.VMEM((width // 128, 3 * height, 128), jnp.float32),
            pltpu.VMEM((3, width // 128, 3 * height, 128), jnp.float32),
            pltpu.VMEM((width // 128, 6, 8, 128), jnp.float32),
            pltpu.VMEM((width // 128, 6, 8, 128), jnp.float32),
            pltpu.VMEM((4, width // 128, 6, 8, 128), jnp.float32),
        ],
        in_specs=[pl.BlockSpec(memory_space=pltpu.SMEM)] + [pl.BlockSpec(memory_space=pltpu.VMEM)] * 6,
        compiler_params=pltpu.CompilerParams(vmem_limit_bytes=32 * 1024 * 1024),
        name="propagate",
    )(parity, cells, drift, diffusivity, rate, inner, outer)


def solve_kernel(terms, rate, points):
    intervals, length = terms.shape[0], 8
    chains = intervals // length
    powers = [jnp.exp(-rate[...])]
    for _ in range(length - 1):
        powers.append(powers[-1] * powers[0])
    sums = [[terms[c * length]] for c in range(chains)]
    for k in range(1, length):
        for c in range(chains):
            sums[c].append(powers[0] * sums[c][-1] + terms[c * length + k])
    jump = powers[-1]
    closing, whole = sums[0][-1], jump
    for c in range(1, chains):
        closing = jump * closing + sums[c][-1]
        whole = whole * jump
    carry = closing / (1.0 - whole)
    for c in range(chains):
        for k in range(length):
            points[(c * length + k + 2) % intervals] = powers[k] * carry + sums[c][k]
        carry = jump * carry + sums[c][-1]


def coarse_solve(terms, rate):
    return pl.pallas_call(
        solve_kernel,
        out_shape=jax.ShapeDtypeStruct(terms.shape, jnp.float32),
        compiler_params=pltpu.CompilerParams(vmem_limit_bytes=2 * 1024 * 1024),
        name="coarse_solve",
    )(terms, rate)


def passed_along(value, axis, steps):
    count = lax.axis_size(axis)
    return lax.ppermute(value, axis, [(i, (i + steps) % count) for i in range(count)])


def to_tiles(value):
    height, width = value.shape
    return value.reshape(height // 8, 8, width // 128, 128).transpose(0, 2, 1, 3).reshape(-1, 8, 128)


def from_tiles(value, height, width):
    return value.reshape(height // 8, width // 128, 8, 128).transpose(0, 2, 1, 3).reshape(height, width)


def shards(cstates, drift, diffusivity, coarse_rate):
    cells = cstates[0]
    height, width = cells.shape
    message = jnp.concatenate([cells, drift[0], drift[1], diffusivity], axis=0)
    strips = lax.axis_size("space")
    outer = lax.ppermute(message, "space", [(i, (((i + 1) ^ 1) - 1) % strips) for i in range(strips)])
    inner = lax.ppermute(message, "space", [(i, i ^ 1) for i in range(strips)])
    parity = (lax.axis_index("space") % 2).reshape(1)
    second, first, term = propagate(parity, cells, drift, diffusivity, coarse_rate, inner, outer)
    rate = lax.dynamic_index_in_dim(to_tiles(coarse_rate), lax.axis_index("tm"), 0, keepdims=False)
    ahead = passed_along(second, "tm", 1) - first
    residual = passed_along(ahead, "tm", 1)
    terms = lax.all_to_all(term, "tm", 0, 0, tiled=True)
    points = coarse_solve(terms, rate)
    points = lax.all_to_all(points, "tm", 0, 0, tiled=True)
    cpoints = from_tiles(points, height, width)
    return cpoints[None], residual[None]


def solution(mesh):
    placed = (P("tm", "space", None), P(None, "space", None), P("space", None), P("space", None))
    return jax.shard_map(
        shards,
        mesh=mesh,
        in_specs=placed,
        out_specs=(P("tm", "space", None), P("tm", "space", None)),
        check_vma=False,
    )
```

```python
import jax
import jax.numpy as jnp
from jax import lax
from jax.experimental import pallas as pl
from jax.experimental.pallas import tpu as pltpu
from jax.sharding import PartitionSpec as P

M = 8
nonlinear_weight = 0.05


def load_interleaved(dst, source, first, blocks):
    for c in range(source.shape[0]):
        for i in range(blocks):
            dst[c, i] = source[c, pl.ds(first + i, 8, stride=blocks), :]


def steps(state, other, coefs, blocks):
    tiles = state.shape[0]
    lane = lax.broadcasted_iota(jnp.int32, (8, 128), 1)
    is_last, is_first = lane == 127, lane == 0

    def one(src, dst):
        for i in range(blocks):
            to_left = lambda c: pltpu.roll(src[c % tiles, i], 127, 1)
            to_right = lambda c: pltpu.roll(src[c % tiles, i], 1, 1)
            ahead, behind, here = to_left(0), to_right(-1), to_right(0)
            for c in range(tiles):
                u = src[c, i]
                above = src[c, i + 1] if i + 1 < blocks else pltpu.roll(src[c, 0], 7, 0)
                below = src[c, i - 1] if i > 0 else pltpu.roll(src[c, blocks - 1], 1, 0)
                following = to_left(c + 1)
                right = jnp.where(is_last, following, ahead)
                left = jnp.where(is_first, behind, here)
                ahead, behind, here = following, here, to_right(c + 1)
                spread = coefs[2, c, i] * ((above + below) + (right + left))
                along = (coefs[0, c, i] + (0.5 * nonlinear_weight) * u) * (right - left)
                across = coefs[1, c, i] * (above - below)
                dst[c, i] = ((coefs[3, c, i] * u + spread) - along) - across

    def pair(_, carry):
        one(state, other)
        one(other, state)
        return carry

    lax.fori_loop(0, M // 2, pair, 0)


def propagate_kernel(
    parity, cells, drift, diffusivity, rate, outer, inner, second_out, first_out, term_out, rows, coef_rows, state, other, coefs
):
    height, width = cells.shape
    tiles = width // 128
    def gather(before, after):
        for c in range(tiles):
            cols = slice(c * 128, c * 128 + 128)
            rows[c, 0:height] = before[0:height, cols]
            rows[c, height : 2 * height] = cells[:, cols]
            rows[c, 2 * height :] = after[0:height, cols]
            for k in range(3):
                scale = 0.5 if k < 2 else 1.0
                own = drift[k, :, cols] if k < 2 else diffusivity[:, cols]
                part = slice((k + 1) * height, (k + 2) * height)
                coef_rows[k, c, 0:height] = scale * before[part, cols]
                coef_rows[k, c, height : 2 * height] = scale * own
                coef_rows[k, c, 2 * height :] = scale * after[part, cols]

    @pl.when(parity[0] == 0)
    def _():
        gather(outer, inner)

    @pl.when(parity[0] == 1)
    def _():
        gather(inner, outer)

    def phase(first, blocks, out):
        load_interleaved(state, rows, first, blocks)
        for k in range(3):
            load_interleaved(coefs.at[k], coef_rows.at[k], first, blocks)
        for c in range(tiles):
            for i in range(blocks):
                coefs[3, c, i] = 1.0 - 4.0 * coefs[2, c, i]
        steps(state, other, coefs, blocks)
        for c in range(tiles):
            for i in range(blocks):
                rows[c, pl.ds(first + i, 8, stride=blocks), :] = state[c, i]
        for c in range(tiles):
            out[:, c * 128 : c * 128 + 128] = rows[c, height : 2 * height]

    phase(0, 6, first_out)
    phase(8, 4, second_out)
    for r in range(height // 8):
        for c in range(tiles):
            part = (slice(r * 8, r * 8 + 8), slice(c * 128, c * 128 + 128))
            term_out[r * tiles + c] = second_out[part] - jnp.exp(-rate[part]) * first_out[part]


def propagate(parity, cells, drift, diffusivity, rate, outer, inner):
    height, width = cells.shape
    tiles = height // 8 * (width // 128)
    shape = lambda *s: jax.ShapeDtypeStruct(s, jnp.float32)
    return pl.pallas_call(
        propagate_kernel,
        out_shape=(shape(height, width), shape(height, width), shape(tiles, 8, 128)),
        scratch_shapes=[
            pltpu.VMEM((width // 128, 3 * height, 128), jnp.float32),
            pltpu.VMEM((3, width // 128, 3 * height, 128), jnp.float32),
            pltpu.VMEM((width // 128, 6, 8, 128), jnp.float32),
            pltpu.VMEM((width // 128, 6, 8, 128), jnp.float32),
            pltpu.VMEM((4, width // 128, 6, 8, 128), jnp.float32),
        ],
        in_specs=[pl.BlockSpec(memory_space=pltpu.SMEM)] + [pl.BlockSpec(memory_space=pltpu.VMEM)] * 6,
        compiler_params=pltpu.CompilerParams(vmem_limit_bytes=32 * 1024 * 1024),
        name="propagate",
    )(parity, cells, drift, diffusivity, rate, outer, inner)


def solve_kernel(terms, rate, points):
    intervals, length = terms.shape[0], 8
    chains = intervals // length
    powers = [jnp.exp(-rate[...])]
    for _ in range(length - 1):
        powers.append(powers[-1] * powers[0])
    sums = [[terms[c * length]] for c in range(chains)]
    for k in range(1, length):
        for c in range(chains):
            sums[c].append(powers[0] * sums[c][-1] + terms[c * length + k])
    jump = powers[-1]
    closing, whole = sums[0][-1], jump
    for c in range(1, chains):
        closing = jump * closing + sums[c][-1]
        whole = whole * jump
    carry = closing / (1.0 - whole)
    for c in range(chains):
        for k in range(length):
            points[(c * length + k + 2) % intervals] = powers[k] * carry + sums[c][k]
        carry = jump * carry + sums[c][-1]


def coarse_solve(terms, rate):
    return pl.pallas_call(
        solve_kernel,
        out_shape=jax.ShapeDtypeStruct(terms.shape, jnp.float32),
        compiler_params=pltpu.CompilerParams(vmem_limit_bytes=2 * 1024 * 1024),
        name="coarse_solve",
    )(terms, rate)


def passed_along(value, axis, steps):
    count = lax.axis_size(axis)
    return lax.ppermute(value, axis, [(i, (i + steps) % count) for i in range(count)])


def to_tiles(value):
    height, width = value.shape
    return value.reshape(height // 8, 8, width // 128, 128).transpose(0, 2, 1, 3).reshape(-1, 8, 128)


def from_tiles(value, height, width):
    return value.reshape(height // 8, width // 128, 8, 128).transpose(0, 2, 1, 3).reshape(height, width)


def shards(cstates, drift, diffusivity, coarse_rate):
    cells = cstates[0]
    height, width = cells.shape
    message = jnp.concatenate([cells, drift.reshape(-1, width), diffusivity], axis=0)
    strips = lax.axis_size("space")
    inner = lax.ppermute(message, "space", [(i, i ^ 1) for i in range(strips)])
    outer = lax.ppermute(message, "space", [(i, (((i + 1) ^ 1) - 1) % strips) for i in range(strips)])
    parity = (lax.axis_index("space") % 2).reshape(1)
    second, first, term = propagate(parity, cells, drift, diffusivity, coarse_rate, outer, inner)
    rate = lax.dynamic_index_in_dim(to_tiles(coarse_rate), lax.axis_index("tm"), 0, keepdims=False)
    terms = lax.all_to_all(term, "tm", 0, 0, tiled=True)
    moved = passed_along(second, "tm", 1)
    terms, moved = lax.optimization_barrier((terms, moved))
    points = coarse_solve(terms, rate)
    points = lax.all_to_all(points, "tm", 0, 0, tiled=True)
    residual = passed_along(moved - first, "tm", 1)
    cpoints = from_tiles(points, height, width)
    return cpoints[None], residual[None]


def solution(mesh):
    placed = (P("tm", "space", None), P(None, "space", None), P("space", None), P("space", None))
    return jax.shard_map(
        shards,
        mesh=mesh,
        in_specs=placed,
        out_specs=(P("tm", "space", None), P("tm", "space", None)),
        check_vma=False,
    )
```

```python
import jax
import jax.numpy as jnp
from jax import lax
from jax.experimental import pallas as pl
from jax.experimental.pallas import tpu as pltpu
from jax.sharding import PartitionSpec as P

M = 8
nonlinear_weight = 0.05


def store_kernel(value, out, sem):
    copy = pltpu.make_async_copy(value, out, sem)
    copy.start()
    copy.wait()


def store(value):
    return pl.pallas_call(
        store_kernel,
        out_shape=jax.ShapeDtypeStruct(value.shape, jnp.float32),
        in_specs=[pl.BlockSpec(memory_space=pltpu.VMEM)],
        out_specs=pl.BlockSpec(memory_space=pl.ANY),
        scratch_shapes=[pltpu.SemaphoreType.DMA],
        compiler_params=pltpu.CompilerParams(vmem_limit_bytes=2 * 1024 * 1024),
        name="store",
    )(value)


def next_cell(u, above, below, right, left, coefs):
    spread = coefs[2] * ((above + below) + (right + left))
    along = (coefs[0] + (0.5 * nonlinear_weight) * u) * (right - left)
    across = coefs[1] * (above - below)
    return ((coefs[3] * u + spread) - along) - across


def load_state(strips, rows):
    tiles = rows.shape[0]
    for c in range(tiles):
        for k, strip in enumerate(strips):
            for r in range(2):
                rows[c, k * 16 + r * 8 : k * 16 + r * 8 + 8] = strip[r * tiles + c]


def load_coefs(strips, coef_rows):
    tiles = coef_rows.shape[1]
    for c in range(tiles):
        for k, strip in enumerate(strips):
            for r in range(2):
                place = slice(k * 16 + r * 8, k * 16 + r * 8 + 8)
                parts = [strip[(2 * f + r) * tiles + c] for f in (1, 2, 3)]
                coef_rows[0, c, place] = 0.5 * parts[0]
                coef_rows[1, c, place] = 0.5 * parts[1]
                coef_rows[2, c, place] = parts[2]
                coef_rows[3, c, place] = 1.0 - 4.0 * parts[2]


def near_kernel(parity, own, inner, history, first_half, rows, coef_rows, state, other, coefs):
    tiles, blocks = state.shape[0], state.shape[1]
    lane = lax.broadcasted_iota(jnp.int32, (8, 128), 1)
    is_last, is_first = lane == 127, lane == 0

    def one(src, dst):
        for i in range(blocks):
            to_left = lambda c: pltpu.roll(src[c % tiles, i], 127, 1)
            to_right = lambda c: pltpu.roll(src[c % tiles, i], 1, 1)
            ahead, behind, here = to_left(0), to_right(-1), to_right(0)
            for c in range(tiles):
                u = src[c, i]
                above = src[c, i + 1] if i + 1 < blocks else pltpu.roll(src[c, 0], 7, 0)
                below = src[c, i - 1] if i > 0 else pltpu.roll(src[c, blocks - 1], 1, 0)
                following = to_left(c + 1)
                right = jnp.where(is_last, following, ahead)
                left = jnp.where(is_first, behind, here)
                ahead, behind, here = following, here, to_right(c + 1)
                dst[c, i] = next_cell(u, above, below, right, left, [coefs[f, c, i] for f in range(4)])

    def run(strips, inner_is_after):
        load_coefs(strips, coef_rows)
        load_state(strips, rows)
        for c in range(tiles):
            for i in range(blocks):
                place = pl.ds(i, 8, stride=blocks)
                state[c, i] = rows[c, place, :]
                for f in range(4):
                    coefs[f, c, i] = coef_rows[f, c, place, :]

        def group(g, carry):
            for j in range(blocks):
                src, dst = (state, other) if j % 2 == 0 else (other, state)
                for w in range(2):
                    sub, block = divmod(j + w, blocks)
                    if inner_is_after:
                        row = (block, g + sub)
                    else:
                        row = (blocks - 1 - block, 7 - g - sub)
                    for c in range(tiles):
                        history[blocks * g + j, w, c : c + 1] = src[c, row[0], pl.ds(row[1], 1), :]
                one(src, dst)

            @pl.when(g == M // blocks - 1)
            def _():
                for c in range(tiles):
                    for i in range(blocks):
                        rows[c, pl.ds(i, 8, stride=blocks), :] = state[c, i]
                start = M if inner_is_after else 2 * M
                for c in range(tiles):
                    first_half[:, c * 128 : c * 128 + 128] = rows[c, start : start + M]

            return carry

        lax.fori_loop(0, 2 * M // blocks, group, 0)

    @pl.when(parity[0] == 0)
    def _():
        run((own, inner), True)

    @pl.when(parity[0] == 1)
    def _():
        run((inner, own), False)


def near(parity, own, inner):
    height, tiles = 16, own.shape[0] // 8
    width = tiles * 128
    return pl.pallas_call(
        near_kernel,
        out_shape=(
            jax.ShapeDtypeStruct((2 * M, 2, tiles, 128), jnp.float32),
            jax.ShapeDtypeStruct((M, width), jnp.float32),
        ),
        scratch_shapes=[
            pltpu.VMEM((tiles, 2 * height, 128), jnp.float32),
            pltpu.VMEM((4, tiles, 2 * height, 128), jnp.float32),
            pltpu.VMEM((tiles, 4, 8, 128), jnp.float32),
            pltpu.VMEM((tiles, 4, 8, 128), jnp.float32),
            pltpu.VMEM((4, tiles, 4, 8, 128), jnp.float32),
        ],
        in_specs=[pl.BlockSpec(memory_space=pltpu.SMEM)] + [pl.BlockSpec(memory_space=pltpu.VMEM)] * 2,
        compiler_params=pltpu.CompilerParams(vmem_limit_bytes=16 * 1024 * 1024),
        cost_estimate=pl.CostEstimate(flops=0, bytes_accessed=0, transcendentals=0),
        name="near",
    )(parity, own, inner)


def far_kernel(
    parity, own, rate, outer, history, first_half, second_out, first_out, term_out, rows, coef_rows, state, other
):
    tiles = state.shape[0]
    lane = lax.broadcasted_iota(jnp.int32, (8, 128), 1)
    is_last, is_first = lane == 127, lane == 0
    sub = lax.broadcasted_iota(jnp.int32, (8, 128), 0)

    def one(k, src, dst, outer_is_before):
        def column(c):
            c = c % tiles
            even, odd = src[c, 0], src[c, 1]
            joins = [jnp.broadcast_to(history[k, w, c : c + 1], (8, 128)) for w in range(2)]
            if outer_is_before:
                even_on = jnp.where(sub == 7, joins[0], pltpu.roll(even, 7, 0))
                odd_on = jnp.where(sub == 7, joins[1], pltpu.roll(odd, 7, 0))
                cells = [(odd, even_on, even), (even_on, odd_on, odd)]
            else:
                even_on = jnp.where(sub == 0, joins[1], pltpu.roll(even, 1, 0))
                odd_on = jnp.where(sub == 0, joins[0], pltpu.roll(odd, 1, 0))
                cells = [(odd_on, even, even_on), (even, odd, odd_on)]
            return cells, [pltpu.roll(u, 127, 1) for u, _, _ in cells], [pltpu.roll(u, 1, 1) for u, _, _ in cells]

        behind, here = column(-1), column(0)
        top = k + 1 if outer_is_before else 2 * M - 1 - k
        for c in range(tiles):
            ahead = column(c + 1)
            for i in range(2):
                u, above, below = here[0][i]
                right = jnp.where(is_last, ahead[1][i], here[1][i])
                left = jnp.where(is_first, behind[2][i], here[2][i])
                place = pl.ds(top + i, 8, stride=2)
                dst[c, i] = next_cell(u, above, below, right, left, [coef_rows[f, c, place, :] for f in range(4)])
            behind, here = here, ahead

    def unfold():
        for c in range(tiles):
            for i in range(2):
                rows[c, pl.ds(i, 8, stride=2), :] = state[c, i]

    def run(strips, outer_is_before):
        load_coefs(strips, coef_rows)
        load_state((outer,), rows)
        for c in range(tiles):
            for i in range(2):
                state[c, i] = rows[c, pl.ds(i, 8, stride=2), :]

        def pair(h, carry):
            @pl.when(h == M // 2)
            def _():
                unfold()
                for c in range(tiles):
                    cols = slice(c * 128, c * 128 + 128)
                    if outer_is_before:
                        first_out[0:M, cols] = rows[c, M : 2 * M]
                        first_out[M : 2 * M, cols] = first_half[:, cols]
                    else:
                        first_out[0:M, cols] = first_half[:, cols]
                        first_out[M : 2 * M, cols] = rows[c, 0:M]

            one(2 * h, state, other, outer_is_before)
            one(2 * h + 1, other, state, outer_is_before)
            return carry

        lax.fori_loop(0, M, pair, 0)

    @pl.when(parity[0] == 0)
    def _():
        run((outer, own), True)

    @pl.when(parity[0] == 1)
    def _():
        run((own, outer), False)

    unfold()
    for c in range(tiles):
        cols = slice(c * 128, c * 128 + 128)
        second_out[:, cols] = rows[c]
        for r in range(2):
            part = (slice(r * 8, r * 8 + 8), cols)
            term_out[r * tiles + c] = rows[c, r * 8 : r * 8 + 8] - jnp.exp(-rate[part]) * first_out[part]


def far(parity, own, rate, outer, history, first_half):
    height, width = rate.shape
    tiles = width // 128
    shape = lambda *s: jax.ShapeDtypeStruct(s, jnp.float32)
    return pl.pallas_call(
        far_kernel,
        out_shape=(shape(height, width), shape(height, width), shape(2 * tiles, 8, 128)),
        scratch_shapes=[
            pltpu.VMEM((tiles, height, 128), jnp.float32),
            pltpu.VMEM((4, tiles, 2 * height, 128), jnp.float32),
            pltpu.VMEM((tiles, 2, 8, 128), jnp.float32),
            pltpu.VMEM((tiles, 2, 8, 128), jnp.float32),
        ],
        in_specs=[pl.BlockSpec(memory_space=pltpu.SMEM)] + [pl.BlockSpec(memory_space=pltpu.VMEM)] * 5,
        compiler_params=pltpu.CompilerParams(vmem_limit_bytes=16 * 1024 * 1024),
        name="far",
    )(parity, own, rate, outer, history, first_half)


def solve_kernel(terms, rate, points):
    intervals, length = terms.shape[0], 8
    chains = intervals // length
    powers = [jnp.exp(-rate[...])]
    for _ in range(length - 1):
        powers.append(powers[-1] * powers[0])
    sums = [[terms[c * length]] for c in range(chains)]
    for k in range(1, length):
        for c in range(chains):
            sums[c].append(powers[0] * sums[c][-1] + terms[c * length + k])
    jump = powers[-1]
    closing, whole = sums[0][-1], jump
    for c in range(1, chains):
        closing = jump * closing + sums[c][-1]
        whole = whole * jump
    carry = closing / (1.0 - whole)
    for c in range(chains):
        for k in range(length):
            points[(c * length + k + 2) % intervals] = powers[k] * carry + sums[c][k]
        carry = jump * carry + sums[c][-1]


def coarse_solve(terms, rate):
    return pl.pallas_call(
        solve_kernel,
        out_shape=jax.ShapeDtypeStruct(terms.shape, jnp.float32),
        compiler_params=pltpu.CompilerParams(vmem_limit_bytes=2 * 1024 * 1024),
        name="coarse_solve",
    )(terms, rate)


def passed_along(value, axis, steps):
    count = lax.axis_size(axis)
    return lax.ppermute(value, axis, [(i, (i + steps) % count) for i in range(count)])


def to_tiles(value):
    height, width = value.shape
    return value.reshape(height // 8, 8, width // 128, 128).transpose(0, 2, 1, 3).reshape(-1, 8, 128)


def from_tiles(value, height, width):
    return value.reshape(height // 8, width // 128, 8, 128).transpose(0, 2, 1, 3).reshape(height, width)


def shards(cstates, drift, diffusivity, coarse_rate):
    cells = cstates[0]
    height, width = cells.shape
    parts = [to_tiles(cells), to_tiles(drift.reshape(-1, width)), to_tiles(diffusivity)]
    message = jnp.concatenate(parts)
    strips = lax.axis_size("space")
    inner = lax.ppermute(message, "space", [(i, i ^ 1) for i in range(strips)])
    outer = lax.ppermute(jnp.concatenate(parts + [jnp.zeros((1, 8, 128), jnp.float32)]), "space", [(i, (((i + 1) ^ 1) - 1) % strips) for i in range(strips)])
    parity = (lax.axis_index("space") % 2).reshape(1)
    history, first_half = near(parity, message, inner)
    second, first, term = far(parity, message, coarse_rate, outer, history, first_half)
    rate = lax.dynamic_index_in_dim(to_tiles(coarse_rate), lax.axis_index("tm"), 0, keepdims=False)
    terms = lax.all_to_all(term, "tm", 0, 0, tiled=True)
    moved = passed_along(second, "tm", 1)
    terms, moved = lax.optimization_barrier((terms, moved))
    points = coarse_solve(terms, rate)
    points = lax.all_to_all(points, "tm", 0, 0, tiled=True)
    residual = store(passed_along(moved - first, "tm", 1))
    cpoints = from_tiles(points, height, width)
    return cpoints[None], residual[None]


def solution(mesh):
    placed = (P("tm", "space", None), P(None, "space", None), P("space", None), P("space", None))
    return jax.shard_map(
        shards,
        mesh=mesh,
        in_specs=placed,
        out_specs=(P("tm", "space", None), P("tm", "space", None)),
        check_vma=False,
    )
```

```python
import jax
import jax.numpy as jnp
from jax import lax
from jax.experimental import pallas as pl
from jax.experimental.pallas import tpu as pltpu
from jax.sharding import PartitionSpec as P

M = 8
nonlinear_weight = 0.05


def store_kernel(value, out, sem):
    copy = pltpu.make_async_copy(value, out, sem)
    copy.start()
    copy.wait()


def store(value):
    return pl.pallas_call(
        store_kernel,
        out_shape=jax.ShapeDtypeStruct(value.shape, jnp.float32),
        in_specs=[pl.BlockSpec(memory_space=pltpu.VMEM)],
        out_specs=pl.BlockSpec(memory_space=pl.ANY),
        scratch_shapes=[pltpu.SemaphoreType.DMA],
        compiler_params=pltpu.CompilerParams(vmem_limit_bytes=2 * 1024 * 1024),
        name="store",
    )(value)


def next_cell(u, above, below, right, left, coefs):
    spread = coefs[2] * ((above + below) + (right + left))
    along = (coefs[0] + (0.5 * nonlinear_weight) * u) * (right - left)
    across = coefs[1] * (above - below)
    return ((coefs[3] * u + spread) - along) - across


def load_state(strips, rows):
    tiles = rows.shape[0]
    for c in range(tiles):
        for k, strip in enumerate(strips):
            for r in range(2):
                rows[c, k * 16 + r * 8 : k * 16 + r * 8 + 8] = strip[r * tiles + c]


def load_coefs(strips, coef_rows):
    tiles = coef_rows.shape[1]
    for c in range(tiles):
        for k, strip in enumerate(strips):
            for r in range(2):
                place = slice(k * 16 + r * 8, k * 16 + r * 8 + 8)
                parts = [strip[(2 * f + r) * tiles + c] for f in (1, 2, 3)]
                coef_rows[0, c, place] = 0.5 * parts[0]
                coef_rows[1, c, place] = 0.5 * parts[1]
                coef_rows[2, c, place] = parts[2]
                coef_rows[3, c, place] = 1.0 - 4.0 * parts[2]


def near_kernel(parity, own, inner, history, first_half, rows, coef_rows, state, other, coefs):
    tiles, blocks = state.shape[0], state.shape[1]
    lane = lax.broadcasted_iota(jnp.int32, (8, 128), 1)
    is_last, is_first = lane == 127, lane == 0

    def one(src, dst):
        for i in range(blocks):
            to_left = lambda c: pltpu.roll(src[c % tiles, i], 127, 1)
            to_right = lambda c: pltpu.roll(src[c % tiles, i], 1, 1)
            ahead, behind, here = to_left(0), to_right(-1), to_right(0)
            for c in range(tiles):
                u = src[c, i]
                above = src[c, i + 1] if i + 1 < blocks else pltpu.roll(src[c, 0], 7, 0)
                below = src[c, i - 1] if i > 0 else pltpu.roll(src[c, blocks - 1], 1, 0)
                following = to_left(c + 1)
                right = jnp.where(is_last, following, ahead)
                left = jnp.where(is_first, behind, here)
                ahead, behind, here = following, here, to_right(c + 1)
                dst[c, i] = next_cell(u, above, below, right, left, [coefs[f, c, i] for f in range(4)])

    def run(strips, inner_is_after):
        load_coefs(strips, coef_rows)
        load_state(strips, rows)
        for c in range(tiles):
            for i in range(blocks):
                place = pl.ds(i, 8, stride=blocks)
                state[c, i] = rows[c, place, :]
                for f in range(4):
                    coefs[f, c, i] = coef_rows[f, c, place, :]

        def group(g, carry):
            for j in range(blocks):
                src, dst = (state, other) if j % 2 == 0 else (other, state)
                for w in range(2):
                    sub, block = divmod(j + w, blocks)
                    if inner_is_after:
                        row = (block, g + sub)
                    else:
                        row = (blocks - 1 - block, 7 - g - sub)
                    for c in range(tiles):
                        history[blocks * g + j, w, c : c + 1] = src[c, row[0], pl.ds(row[1], 1), :]
                one(src, dst)

            @pl.when(g == M // blocks - 1)
            def _():
                for c in range(tiles):
                    for i in range(blocks):
                        rows[c, pl.ds(i, 8, stride=blocks), :] = state[c, i]
                start = M if inner_is_after else 2 * M
                for c in range(tiles):
                    first_half[:, c * 128 : c * 128 + 128] = rows[c, start : start + M]

            return carry

        lax.fori_loop(0, 2 * M // blocks, group, 0)

    @pl.when(parity[0] == 0)
    def _():
        run((own, inner), True)

    @pl.when(parity[0] == 1)
    def _():
        run((inner, own), False)


def near(parity, own, inner):
    height, tiles = 16, own.shape[0] // 8
    width = tiles * 128
    return pl.pallas_call(
        near_kernel,
        out_shape=(
            jax.ShapeDtypeStruct((2 * M, 2, tiles, 128), jnp.float32),
            jax.ShapeDtypeStruct((M, width), jnp.float32),
        ),
        scratch_shapes=[
            pltpu.VMEM((tiles, 2 * height, 128), jnp.float32),
            pltpu.VMEM((4, tiles, 2 * height, 128), jnp.float32),
            pltpu.VMEM((tiles, 4, 8, 128), jnp.float32),
            pltpu.VMEM((tiles, 4, 8, 128), jnp.float32),
            pltpu.VMEM((4, tiles, 4, 8, 128), jnp.float32),
        ],
        in_specs=[pl.BlockSpec(memory_space=pltpu.SMEM)] + [pl.BlockSpec(memory_space=pltpu.VMEM)] * 2,
        compiler_params=pltpu.CompilerParams(vmem_limit_bytes=16 * 1024 * 1024),
        cost_estimate=pl.CostEstimate(flops=0, bytes_accessed=0, transcendentals=0),
        name="near",
    )(parity, own, inner)


def far_kernel(
    parity, own, rate, outer, history, first_half, second_out, first_out, term_out, rows, coef_rows, state, other
):
    tiles = state.shape[0]
    lane = lax.broadcasted_iota(jnp.int32, (8, 128), 1)
    is_last, is_first = lane == 127, lane == 0
    sub = lax.broadcasted_iota(jnp.int32, (8, 128), 0)

    def one(k, src, dst, outer_is_before):
        def column(c):
            c = c % tiles
            even, odd = src[c, 0], src[c, 1]
            joins = [jnp.broadcast_to(history[k, w, c : c + 1], (8, 128)) for w in range(2)]
            if outer_is_before:
                even_on = jnp.where(sub == 7, joins[0], pltpu.roll(even, 7, 0))
                odd_on = jnp.where(sub == 7, joins[1], pltpu.roll(odd, 7, 0))
                cells = [(odd, even_on, even), (even_on, odd_on, odd)]
            else:
                even_on = jnp.where(sub == 0, joins[1], pltpu.roll(even, 1, 0))
                odd_on = jnp.where(sub == 0, joins[0], pltpu.roll(odd, 1, 0))
                cells = [(odd_on, even, even_on), (even, odd, odd_on)]
            return cells, [pltpu.roll(u, 127, 1) for u, _, _ in cells], [pltpu.roll(u, 1, 1) for u, _, _ in cells]

        behind, here = column(-1), column(0)
        top = k + 1 if outer_is_before else 2 * M - 1 - k
        for c in range(tiles):
            ahead = column(c + 1)
            for i in range(2):
                u, above, below = here[0][i]
                right = jnp.where(is_last, ahead[1][i], here[1][i])
                left = jnp.where(is_first, behind[2][i], here[2][i])
                place = pl.ds(top + i, 8, stride=2)
                dst[c, i] = next_cell(u, above, below, right, left, [coef_rows[f, c, place, :] for f in range(4)])
            behind, here = here, ahead

    def unfold():
        for c in range(tiles):
            for i in range(2):
                rows[c, pl.ds(i, 8, stride=2), :] = state[c, i]

    def run(strips, outer_is_before):
        load_coefs(strips, coef_rows)
        load_state((outer,), rows)
        for c in range(tiles):
            for i in range(2):
                state[c, i] = rows[c, pl.ds(i, 8, stride=2), :]

        def pair(h, carry):
            @pl.when(h == M // 2)
            def _():
                unfold()
                for c in range(tiles):
                    cols = slice(c * 128, c * 128 + 128)
                    if outer_is_before:
                        first_out[0:M, cols] = rows[c, M : 2 * M]
                        first_out[M : 2 * M, cols] = first_half[:, cols]
                    else:
                        first_out[0:M, cols] = first_half[:, cols]
                        first_out[M : 2 * M, cols] = rows[c, 0:M]

            one(2 * h, state, other, outer_is_before)
            one(2 * h + 1, other, state, outer_is_before)
            return carry

        lax.fori_loop(0, M, pair, 0)

    @pl.when(parity[0] == 0)
    def _():
        run((outer, own), True)

    @pl.when(parity[0] == 1)
    def _():
        run((own, outer), False)

    unfold()
    for c in range(tiles):
        cols = slice(c * 128, c * 128 + 128)
        second_out[:, cols] = rows[c]
        for r in range(2):
            part = (slice(r * 8, r * 8 + 8), cols)
            term_out[r * tiles + c] = rows[c, r * 8 : r * 8 + 8] - jnp.exp(-rate[part]) * first_out[part]


def far(parity, own, rate, outer, history, first_half):
    height, width = rate.shape
    tiles = width // 128
    shape = lambda *s: jax.ShapeDtypeStruct(s, jnp.float32)
    return pl.pallas_call(
        far_kernel,
        out_shape=(shape(height, width), shape(height, width), shape(2 * tiles, 8, 128)),
        scratch_shapes=[
            pltpu.VMEM((tiles, height, 128), jnp.float32),
            pltpu.VMEM((4, tiles, 2 * height, 128), jnp.float32),
            pltpu.VMEM((tiles, 2, 8, 128), jnp.float32),
            pltpu.VMEM((tiles, 2, 8, 128), jnp.float32),
        ],
        in_specs=[pl.BlockSpec(memory_space=pltpu.SMEM)] + [pl.BlockSpec(memory_space=pltpu.VMEM)] * 5,
        compiler_params=pltpu.CompilerParams(vmem_limit_bytes=16 * 1024 * 1024),
        name="far",
    )(parity, own, rate, outer, history, first_half)


def solve_kernel(terms, rate, points):
    intervals, length = terms.shape[0], 8
    chains = intervals // length
    powers = [jnp.exp(-rate[...])]
    for _ in range(length - 1):
        powers.append(powers[-1] * powers[0])
    sums = [[terms[c * length]] for c in range(chains)]
    for k in range(1, length):
        for c in range(chains):
            sums[c].append(powers[0] * sums[c][-1] + terms[c * length + k])
    jump = powers[-1]
    closing, whole = sums[0][-1], jump
    for c in range(1, chains):
        closing = jump * closing + sums[c][-1]
        whole = whole * jump
    carry = closing / (1.0 - whole)
    for c in range(chains):
        for k in range(length):
            points[(c * length + k + 2) % intervals] = powers[k] * carry + sums[c][k]
        carry = jump * carry + sums[c][-1]


def coarse_solve(terms, rate):
    return pl.pallas_call(
        solve_kernel,
        out_shape=jax.ShapeDtypeStruct(terms.shape, jnp.float32),
        compiler_params=pltpu.CompilerParams(vmem_limit_bytes=2 * 1024 * 1024),
        name="coarse_solve",
    )(terms, rate)


def passed_along(value, axis, steps):
    count = lax.axis_size(axis)
    return lax.ppermute(value, axis, [(i, (i + steps) % count) for i in range(count)])


def to_tiles(value):
    height, width = value.shape
    return value.reshape(height // 8, 8, width // 128, 128).transpose(0, 2, 1, 3).reshape(-1, 8, 128)


def from_tiles(value, height, width):
    return value.reshape(height // 8, width // 128, 8, 128).transpose(0, 2, 1, 3).reshape(height, width)


def shards(cstates, drift, diffusivity, coarse_rate):
    cells = cstates[0]
    height, width = cells.shape
    parts = [to_tiles(cells), to_tiles(drift.reshape(-1, width)), to_tiles(diffusivity)]
    message = jnp.concatenate(parts)
    strips = lax.axis_size("space")
    inner = lax.ppermute(message, "space", [(i, i ^ 1) for i in range(strips)])
    outer = lax.ppermute(jnp.concatenate(parts + [jnp.zeros((1, 8, 128), jnp.float32)]), "space", [(i, (((i + 1) ^ 1) - 1) % strips) for i in range(strips)])
    parity = (lax.axis_index("space") % 2).reshape(1)
    history, first_half = near(parity, message, inner)
    second, first, term = far(parity, message, coarse_rate, outer, history, first_half)
    rate = lax.dynamic_index_in_dim(to_tiles(coarse_rate), lax.axis_index("tm"), 0, keepdims=False)
    terms = lax.all_to_all(term, "tm", 0, 0, tiled=True)
    second = passed_along(second, "tm", 2)
    first = passed_along(first, "tm", 1)
    points = coarse_solve(terms, rate)
    points = lax.all_to_all(points, "tm", 0, 0, tiled=True)
    residual = second - first
    cpoints = from_tiles(points, height, width)
    return cpoints[None], residual[None]


def solution(mesh):
    placed = (P("tm", "space", None), P(None, "space", None), P("space", None), P("space", None))
    return jax.shard_map(
        shards,
        mesh=mesh,
        in_specs=placed,
        out_specs=(P("tm", "space", None), P("tm", "space", None)),
        check_vma=False,
    )
```

```python
import jax
import jax.numpy as jnp
from jax import lax
from jax.experimental import pallas as pl
from jax.experimental.pallas import tpu as pltpu
from jax.sharding import PartitionSpec as P

M = 8
FIRST = 11
nonlinear_weight = 0.05


def store_kernel(value, out, sem):
    copy = pltpu.make_async_copy(value, out, sem)
    copy.start()
    copy.wait()


def store(value):
    return pl.pallas_call(
        store_kernel,
        out_shape=jax.ShapeDtypeStruct(value.shape, jnp.float32),
        in_specs=[pl.BlockSpec(memory_space=pltpu.VMEM)],
        out_specs=pl.BlockSpec(memory_space=pl.ANY),
        scratch_shapes=[pltpu.SemaphoreType.DMA],
        compiler_params=pltpu.CompilerParams(vmem_limit_bytes=2 * 1024 * 1024),
        name="store",
    )(value)


def next_cell(u, above, below, right, left, coefs):
    spread = coefs[2] * ((above + below) + (right + left))
    along = (coefs[0] + (0.5 * nonlinear_weight) * u) * (right - left)
    across = coefs[1] * (above - below)
    return ((coefs[3] * u + spread) - along) - across


def load_state(strips, rows):
    tiles = rows.shape[0]
    for c in range(tiles):
        for k, strip in enumerate(strips):
            for r in range(2):
                rows[c, k * 16 + r * 8 : k * 16 + r * 8 + 8] = strip[r * tiles + c]


def load_coefs(strips, coef_rows):
    tiles = coef_rows.shape[1]
    for c in range(tiles):
        for k, strip in enumerate(strips):
            for r in range(2):
                place = slice(k * 16 + r * 8, k * 16 + r * 8 + 8)
                parts = [strip[(2 * f + r) * tiles + c] for f in (1, 2, 3)]
                coef_rows[0, c, place] = 0.5 * parts[0]
                coef_rows[1, c, place] = 0.5 * parts[1]
                coef_rows[2, c, place] = parts[2]
                coef_rows[3, c, place] = 1.0 - 4.0 * parts[2]


def near_kernel(parity, own, inner, history, first_half, rows, coef_rows, state, other, coefs):
    tiles, blocks = state.shape[0], state.shape[1]
    lane = lax.broadcasted_iota(jnp.int32, (8, 128), 1)
    is_last, is_first = lane == 127, lane == 0

    def one(src, dst):
        for i in range(blocks):
            to_left = lambda c: pltpu.roll(src[c % tiles, i], 127, 1)
            to_right = lambda c: pltpu.roll(src[c % tiles, i], 1, 1)
            ahead, behind, here = to_left(0), to_right(-1), to_right(0)
            for c in range(tiles):
                u = src[c, i]
                above = src[c, i + 1] if i + 1 < blocks else pltpu.roll(src[c, 0], 7, 0)
                below = src[c, i - 1] if i > 0 else pltpu.roll(src[c, blocks - 1], 1, 0)
                following = to_left(c + 1)
                right = jnp.where(is_last, following, ahead)
                left = jnp.where(is_first, behind, here)
                ahead, behind, here = following, here, to_right(c + 1)
                dst[c, i] = next_cell(u, above, below, right, left, [coefs[f, c, i] for f in range(4)])

    def run(strips, inner_is_after):
        load_coefs(strips, coef_rows)
        load_state(strips, rows)
        for c in range(tiles):
            for i in range(blocks):
                place = pl.ds(i, 8, stride=blocks)
                state[c, i] = rows[c, place, :]
                for f in range(4):
                    coefs[f, c, i] = coef_rows[f, c, place, :]

        def group(g, carry):
            for j in range(blocks):
                src, dst = (state, other) if j % 2 == 0 else (other, state)
                for w in range(2):
                    sub, block = divmod(j + w, blocks)
                    if inner_is_after:
                        row = (block, g + sub)
                    else:
                        row = (blocks - 1 - block, 7 - g - sub)
                    for c in range(tiles):
                        history[blocks * g + j, w, c : c + 1] = src[c, row[0], pl.ds(row[1], 1), :]
                one(src, dst)

            @pl.when(g == M // blocks - 1)
            def _():
                for c in range(tiles):
                    for i in range(blocks):
                        rows[c, pl.ds(i, 8, stride=blocks), :] = state[c, i]
                start = M if inner_is_after else 2 * M
                for c in range(tiles):
                    first_half[:, c * 128 : c * 128 + 128] = rows[c, start : start + M]

            return carry

        lax.fori_loop(0, 2 * M // blocks, group, 0)

    @pl.when(parity[0] == 0)
    def _():
        run((own, inner), True)

    @pl.when(parity[0] == 1)
    def _():
        run((inner, own), False)


def near(parity, own, inner):
    height, tiles = 16, own.shape[0] // 8
    width = tiles * 128
    return pl.pallas_call(
        near_kernel,
        out_shape=(
            jax.ShapeDtypeStruct((2 * M, 2, tiles, 128), jnp.float32),
            jax.ShapeDtypeStruct((M, width), jnp.float32),
        ),
        scratch_shapes=[
            pltpu.VMEM((tiles, 2 * height, 128), jnp.float32),
            pltpu.VMEM((4, tiles, 2 * height, 128), jnp.float32),
            pltpu.VMEM((tiles, 4, 8, 128), jnp.float32),
            pltpu.VMEM((tiles, 4, 8, 128), jnp.float32),
            pltpu.VMEM((4, tiles, 4, 8, 128), jnp.float32),
        ],
        in_specs=[pl.BlockSpec(memory_space=pltpu.SMEM)] + [pl.BlockSpec(memory_space=pltpu.VMEM)] * 2,
        compiler_params=pltpu.CompilerParams(vmem_limit_bytes=16 * 1024 * 1024),
        cost_estimate=pl.CostEstimate(flops=0, bytes_accessed=0, transcendentals=0),
        name="near",
    )(parity, own, inner)


def far_kernel(
    parity, own, rate, outer, history, first_half, second_out, first_out, term_out, rows, coef_rows, state, other
):
    tiles = state.shape[0]
    lane = lax.broadcasted_iota(jnp.int32, (8, 128), 1)
    is_last, is_first = lane == 127, lane == 0
    sub = lax.broadcasted_iota(jnp.int32, (8, 128), 0)

    def one(k, src, dst, outer_is_before):
        def column(c):
            c = c % tiles
            even, odd = src[c, 0], src[c, 1]
            joins = [jnp.broadcast_to(history[k, w, c : c + 1], (8, 128)) for w in range(2)]
            if outer_is_before:
                even_on = jnp.where(sub == 7, joins[0], pltpu.roll(even, 7, 0))
                odd_on = jnp.where(sub == 7, joins[1], pltpu.roll(odd, 7, 0))
                cells = [(odd, even_on, even), (even_on, odd_on, odd)]
            else:
                even_on = jnp.where(sub == 0, joins[1], pltpu.roll(even, 1, 0))
                odd_on = jnp.where(sub == 0, joins[0], pltpu.roll(odd, 1, 0))
                cells = [(odd_on, even, even_on), (even, odd, odd_on)]
            return cells, [pltpu.roll(u, 127, 1) for u, _, _ in cells], [pltpu.roll(u, 1, 1) for u, _, _ in cells]

        behind, here = column(-1), column(0)
        top = k + 1 if outer_is_before else 2 * M - 1 - k
        for c in range(tiles):
            ahead = column(c + 1)
            for i in range(2):
                u, above, below = here[0][i]
                right = jnp.where(is_last, ahead[1][i], here[1][i])
                left = jnp.where(is_first, behind[2][i], here[2][i])
                place = pl.ds(top + i, 8, stride=2)
                dst[c, i] = next_cell(u, above, below, right, left, [coef_rows[f, c, place, :] for f in range(4)])
            behind, here = here, ahead

    def unfold():
        for c in range(tiles):
            for i in range(2):
                rows[c, pl.ds(i, 8, stride=2), :] = state[c, i]

    def run(strips, outer_is_before):
        load_coefs(strips, coef_rows)
        load_state((outer,), rows)
        for c in range(tiles):
            for i in range(2):
                state[c, i] = rows[c, pl.ds(i, 8, stride=2), :]

        def pair(h, carry):
            @pl.when(h == M // 2)
            def _():
                unfold()
                for c in range(tiles):
                    cols = slice(c * 128, c * 128 + 128)
                    if outer_is_before:
                        first_out[0:M, cols] = rows[c, M : 2 * M]
                        first_out[M : 2 * M, cols] = first_half[:, cols]
                    else:
                        first_out[0:M, cols] = first_half[:, cols]
                        first_out[M : 2 * M, cols] = rows[c, 0:M]

            one(2 * h, state, other, outer_is_before)
            one(2 * h + 1, other, state, outer_is_before)
            return carry

        lax.fori_loop(0, M, pair, 0)

    @pl.when(parity[0] == 0)
    def _():
        run((outer, own), True)

    @pl.when(parity[0] == 1)
    def _():
        run((own, outer), False)

    unfold()
    for c in range(tiles):
        cols = slice(c * 128, c * 128 + 128)
        second_out[:, cols] = rows[c]
        for r in range(2):
            part = (slice(r * 8, r * 8 + 8), cols)
            term_out[r * tiles + c] = rows[c, r * 8 : r * 8 + 8] - jnp.exp(-rate[part]) * first_out[part]


def far(parity, own, rate, outer, history, first_half):
    height, width = rate.shape
    tiles = width // 128
    shape = lambda *s: jax.ShapeDtypeStruct(s, jnp.float32)
    return pl.pallas_call(
        far_kernel,
        out_shape=(shape(height, width), shape(height, width), shape(2 * tiles, 8, 128)),
        scratch_shapes=[
            pltpu.VMEM((tiles, height, 128), jnp.float32),
            pltpu.VMEM((4, tiles, 2 * height, 128), jnp.float32),
            pltpu.VMEM((tiles, 2, 8, 128), jnp.float32),
            pltpu.VMEM((tiles, 2, 8, 128), jnp.float32),
        ],
        in_specs=[pl.BlockSpec(memory_space=pltpu.SMEM)] + [pl.BlockSpec(memory_space=pltpu.VMEM)] * 5,
        compiler_params=pltpu.CompilerParams(vmem_limit_bytes=16 * 1024 * 1024),
        name="far",
    )(parity, own, rate, outer, history, first_half)


def solve_kernel(terms, rate, points):
    intervals, length = terms.shape[0], 8
    chains = intervals // length
    powers = [jnp.exp(-rate[...])]
    for _ in range(length - 1):
        powers.append(powers[-1] * powers[0])
    sums = [[terms[c * length]] for c in range(chains)]
    for k in range(1, length):
        for c in range(chains):
            sums[c].append(powers[0] * sums[c][-1] + terms[c * length + k])
    jump = powers[-1]
    closing, whole = sums[0][-1], jump
    for c in range(1, chains):
        closing = jump * closing + sums[c][-1]
        whole = whole * jump
    carry = closing / (1.0 - whole)
    for c in range(chains):
        for k in range(length):
            points[(c * length + k + 2) % intervals] = powers[k] * carry + sums[c][k]
        carry = jump * carry + sums[c][-1]


def coarse_solve(terms, rate):
    return pl.pallas_call(
        solve_kernel,
        out_shape=jax.ShapeDtypeStruct(terms.shape, jnp.float32),
        compiler_params=pltpu.CompilerParams(vmem_limit_bytes=2 * 1024 * 1024),
        name="coarse_solve",
    )(terms, rate)


def passed_along(value, axis, steps):
    count = lax.axis_size(axis)
    return lax.ppermute(value, axis, [(i, (i + steps) % count) for i in range(count)])


def to_tiles(value):
    height, width = value.shape
    return value.reshape(height // 8, 8, width // 128, 128).transpose(0, 2, 1, 3).reshape(-1, 8, 128)


def from_tiles(value, height, width):
    return value.reshape(height // 8, width // 128, 8, 128).transpose(0, 2, 1, 3).reshape(height, width)


def shards(cstates, drift, diffusivity, coarse_rate):
    cells = cstates[0]
    height, width = cells.shape
    parts = [to_tiles(cells), to_tiles(drift.reshape(-1, width)), to_tiles(diffusivity)]
    message = jnp.concatenate(parts)
    strips = lax.axis_size("space")
    inner = lax.ppermute(message, "space", [(i, i ^ 1) for i in range(strips)])
    outer = lax.ppermute(jnp.concatenate(parts + [jnp.zeros((1, 8, 128), jnp.float32)]), "space", [(i, (((i + 1) ^ 1) - 1) % strips) for i in range(strips)])
    parity = (lax.axis_index("space") % 2).reshape(1)
    history, first_half = near(parity, message, inner)
    second, first, term = far(parity, message, coarse_rate, outer, history, first_half)
    count = lax.axis_size("tm")
    ring = [[(k + FIRST) % count for k in range(count)]]
    place = (lax.axis_index("tm") + count - FIRST) % count
    rate = lax.dynamic_index_in_dim(to_tiles(coarse_rate), place, 0, keepdims=False)
    terms = lax.all_to_all(term, "tm", 0, 0, tiled=True, axis_index_groups=ring)
    second = passed_along(second, "tm", 2)
    first = passed_along(first, "tm", 1)
    points = coarse_solve(terms, rate)
    points = lax.all_to_all(points, "tm", 0, 0, tiled=True, axis_index_groups=ring)
    residual = second - first
    cpoints = from_tiles(points, height, width)
    return cpoints[None], residual[None]


def solution(mesh):
    placed = (P("tm", "space", None), P(None, "space", None), P("space", None), P("space", None))
    return jax.shard_map(
        shards,
        mesh=mesh,
        in_specs=placed,
        out_specs=(P("tm", "space", None), P("tm", "space", None)),
        check_vma=False,
    )
```

```python
import jax
import jax.numpy as jnp
from jax import lax
from jax.experimental import pallas as pl
from jax.experimental.pallas import tpu as pltpu
from jax.sharding import PartitionSpec as P

M = 8
FIRST = 11
nonlinear_weight = 0.05


def store_kernel(value, out, sem):
    copy = pltpu.make_async_copy(value, out, sem)
    copy.start()
    copy.wait()


def store(value):
    return pl.pallas_call(
        store_kernel,
        out_shape=jax.ShapeDtypeStruct(value.shape, jnp.float32),
        in_specs=[pl.BlockSpec(memory_space=pltpu.VMEM)],
        out_specs=pl.BlockSpec(memory_space=pl.ANY),
        scratch_shapes=[pltpu.SemaphoreType.DMA],
        compiler_params=pltpu.CompilerParams(vmem_limit_bytes=2 * 1024 * 1024),
        name="store",
    )(value)


def next_cell(u, above, below, right, left, coefs):
    spread = coefs[2] * ((above + below) + (right + left))
    along = (coefs[0] + (0.5 * nonlinear_weight) * u) * (right - left)
    across = coefs[1] * (above - below)
    return ((coefs[3] * u + spread) - along) - across


def load_state(strips, rows):
    tiles = rows.shape[0]
    for c in range(tiles):
        for k, strip in enumerate(strips):
            for r in range(2):
                rows[c, k * 16 + r * 8 : k * 16 + r * 8 + 8] = strip[r * tiles + c]


def load_coefs(strips, coef_rows):
    tiles = coef_rows.shape[1]
    for c in range(tiles):
        for k, strip in enumerate(strips):
            for r in range(2):
                place = slice(k * 16 + r * 8, k * 16 + r * 8 + 8)
                parts = [strip[(2 * f + r) * tiles + c] for f in (1, 2, 3)]
                coef_rows[0, c, place] = 0.5 * parts[0]
                coef_rows[1, c, place] = 0.5 * parts[1]
                coef_rows[2, c, place] = parts[2]
                coef_rows[3, c, place] = 1.0 - 4.0 * parts[2]


def near_kernel(parity, own, inner, history, first_half, rows, coef_rows, state, other, coefs):
    tiles, blocks = state.shape[0], state.shape[1]
    lane = lax.broadcasted_iota(jnp.int32, (8, 128), 1)
    is_last, is_first = lane == 127, lane == 0

    def one(src, dst):
        for i in range(blocks):
            to_left = lambda c: pltpu.roll(src[c % tiles, i], 127, 1)
            to_right = lambda c: pltpu.roll(src[c % tiles, i], 1, 1)
            ahead, behind, here = to_left(0), to_right(-1), to_right(0)
            for c in range(tiles):
                u = src[c, i]
                above = src[c, i + 1] if i + 1 < blocks else pltpu.roll(src[c, 0], 7, 0)
                below = src[c, i - 1] if i > 0 else pltpu.roll(src[c, blocks - 1], 1, 0)
                following = to_left(c + 1)
                right = jnp.where(is_last, following, ahead)
                left = jnp.where(is_first, behind, here)
                ahead, behind, here = following, here, to_right(c + 1)
                dst[c, i] = next_cell(u, above, below, right, left, [coefs[f, c, i] for f in range(4)])

    def run(strips, inner_is_after):
        load_coefs(strips, coef_rows)
        load_state(strips, rows)
        for c in range(tiles):
            for i in range(blocks):
                place = pl.ds(i, 8, stride=blocks)
                state[c, i] = rows[c, place, :]
                for f in range(4):
                    coefs[f, c, i] = coef_rows[f, c, place, :]

        def group(g, carry):
            for j in range(blocks):
                src, dst = (state, other) if j % 2 == 0 else (other, state)
                for w in range(2):
                    sub, block = divmod(j + w, blocks)
                    if inner_is_after:
                        row = (block, g + sub)
                    else:
                        row = (blocks - 1 - block, 7 - g - sub)
                    for c in range(tiles):
                        history[blocks * g + j, w, c : c + 1] = src[c, row[0], pl.ds(row[1], 1), :]
                one(src, dst)

            @pl.when(g == M // blocks - 1)
            def _():
                for c in range(tiles):
                    for i in range(blocks):
                        rows[c, pl.ds(i, 8, stride=blocks), :] = state[c, i]
                start = M if inner_is_after else 2 * M
                for c in range(tiles):
                    first_half[:, c * 128 : c * 128 + 128] = rows[c, start : start + M]

            return carry

        lax.fori_loop(0, 2 * M // blocks, group, 0)

    @pl.when(parity[0] == 0)
    def _():
        run((own, inner), True)

    @pl.when(parity[0] == 1)
    def _():
        run((inner, own), False)


def near(parity, own, inner):
    height, tiles = 16, own.shape[0] // 8
    width = tiles * 128
    return pl.pallas_call(
        near_kernel,
        out_shape=(
            jax.ShapeDtypeStruct((2 * M, 2, tiles, 128), jnp.float32),
            jax.ShapeDtypeStruct((M, width), jnp.float32),
        ),
        scratch_shapes=[
            pltpu.VMEM((tiles, 2 * height + 8, 128), jnp.float32),
            pltpu.VMEM((4, tiles, 2 * height + 8, 128), jnp.float32),
            pltpu.VMEM((tiles, 4, 8, 128), jnp.float32),
            pltpu.VMEM((tiles, 4, 8, 128), jnp.float32),
            pltpu.VMEM((4, tiles, 4, 8, 128), jnp.float32),
        ],
        in_specs=[pl.BlockSpec(memory_space=pltpu.SMEM)] + [pl.BlockSpec(memory_space=pltpu.VMEM)] * 2,
        compiler_params=pltpu.CompilerParams(vmem_limit_bytes=16 * 1024 * 1024),
        cost_estimate=pl.CostEstimate(flops=0, bytes_accessed=0, transcendentals=0),
        name="near",
    )(parity, own, inner)


def far_kernel(
    parity, own, rate, outer, history, first_half, second_out, first_out, term_out, rows, coef_rows, state, other
):
    tiles = state.shape[0]
    lane = lax.broadcasted_iota(jnp.int32, (8, 128), 1)
    is_last, is_first = lane == 127, lane == 0
    sub = lax.broadcasted_iota(jnp.int32, (8, 128), 0)

    def one(k, src, dst, outer_is_before):
        def column(c):
            c = c % tiles
            even, odd = src[c, 0], src[c, 1]
            joins = [jnp.broadcast_to(history[k, w, c : c + 1], (8, 128)) for w in range(2)]
            if outer_is_before:
                even_on = jnp.where(sub == 7, joins[0], pltpu.roll(even, 7, 0))
                odd_on = jnp.where(sub == 7, joins[1], pltpu.roll(odd, 7, 0))
                cells = [(odd, even_on, even), (even_on, odd_on, odd)]
            else:
                even_on = jnp.where(sub == 0, joins[1], pltpu.roll(even, 1, 0))
                odd_on = jnp.where(sub == 0, joins[0], pltpu.roll(odd, 1, 0))
                cells = [(odd_on, even, even_on), (even, odd, odd_on)]
            return cells, [pltpu.roll(u, 127, 1) for u, _, _ in cells], [pltpu.roll(u, 1, 1) for u, _, _ in cells]

        behind, here = column(-1), column(0)
        top = k + 1 if outer_is_before else 2 * M - 1 - k
        for c in range(tiles):
            ahead = column(c + 1)
            for i in range(2):
                u, above, below = here[0][i]
                right = jnp.where(is_last, ahead[1][i], here[1][i])
                left = jnp.where(is_first, behind[2][i], here[2][i])
                place = pl.ds(top + i, 8, stride=2)
                dst[c, i] = next_cell(u, above, below, right, left, [coef_rows[f, c, place, :] for f in range(4)])
            behind, here = here, ahead

    def unfold():
        for c in range(tiles):
            for i in range(2):
                rows[c, pl.ds(i, 8, stride=2), :] = state[c, i]

    def run(strips, outer_is_before):
        load_coefs(strips, coef_rows)
        load_state((outer,), rows)
        for c in range(tiles):
            for i in range(2):
                state[c, i] = rows[c, pl.ds(i, 8, stride=2), :]

        def pair(h, carry):
            @pl.when(h == M // 2)
            def _():
                unfold()
                for c in range(tiles):
                    cols = slice(c * 128, c * 128 + 128)
                    if outer_is_before:
                        first_out[0:M, cols] = rows[c, M : 2 * M]
                        first_out[M : 2 * M, cols] = first_half[:, cols]
                    else:
                        first_out[0:M, cols] = first_half[:, cols]
                        first_out[M : 2 * M, cols] = rows[c, 0:M]

            one(2 * h, state, other, outer_is_before)
            one(2 * h + 1, other, state, outer_is_before)
            return carry

        lax.fori_loop(0, M, pair, 0)

    @pl.when(parity[0] == 0)
    def _():
        run((outer, own), True)

    @pl.when(parity[0] == 1)
    def _():
        run((own, outer), False)

    unfold()
    for c in range(tiles):
        cols = slice(c * 128, c * 128 + 128)
        second_out[:, cols] = rows[c, 0 : 2 * M]
        for r in range(2):
            part = (slice(r * 8, r * 8 + 8), cols)
            term_out[r * tiles + c] = rows[c, r * 8 : r * 8 + 8] - jnp.exp(-rate[part]) * first_out[part]


def far(parity, own, rate, outer, history, first_half):
    height, width = rate.shape
    tiles = width // 128
    shape = lambda *s: jax.ShapeDtypeStruct(s, jnp.float32)
    return pl.pallas_call(
        far_kernel,
        out_shape=(shape(height, width), shape(height, width), shape(2 * tiles, 8, 128)),
        scratch_shapes=[
            pltpu.VMEM((tiles, height + 8, 128), jnp.float32),
            pltpu.VMEM((4, tiles, 2 * height + 8, 128), jnp.float32),
            pltpu.VMEM((tiles, 2, 8, 128), jnp.float32),
            pltpu.VMEM((tiles, 2, 8, 128), jnp.float32),
        ],
        in_specs=[pl.BlockSpec(memory_space=pltpu.SMEM)] + [pl.BlockSpec(memory_space=pltpu.VMEM)] * 5,
        compiler_params=pltpu.CompilerParams(vmem_limit_bytes=16 * 1024 * 1024),
        name="far",
    )(parity, own, rate, outer, history, first_half)


def solve_kernel(terms, rate, points):
    intervals, length = terms.shape[0], 8
    chains = intervals // length
    powers = [jnp.exp(-rate[...])]
    for _ in range(length - 1):
        powers.append(powers[-1] * powers[0])
    sums = [[terms[c * length]] for c in range(chains)]
    for k in range(1, length):
        for c in range(chains):
            sums[c].append(powers[0] * sums[c][-1] + terms[c * length + k])
    jump = powers[-1]
    closing, whole = sums[0][-1], jump
    for c in range(1, chains):
        closing = jump * closing + sums[c][-1]
        whole = whole * jump
    carry = closing / (1.0 - whole)
    for c in range(chains):
        for k in range(length):
            points[(c * length + k + 2) % intervals] = powers[k] * carry + sums[c][k]
        carry = jump * carry + sums[c][-1]


def coarse_solve(terms, rate):
    return pl.pallas_call(
        solve_kernel,
        out_shape=jax.ShapeDtypeStruct(terms.shape, jnp.float32),
        compiler_params=pltpu.CompilerParams(vmem_limit_bytes=2 * 1024 * 1024),
        name="coarse_solve",
    )(terms, rate)


def passed_along(value, axis, steps):
    count = lax.axis_size(axis)
    return lax.ppermute(value, axis, [(i, (i + steps) % count) for i in range(count)])


def to_tiles(value):
    height, width = value.shape
    return value.reshape(height // 8, 8, width // 128, 128).transpose(0, 2, 1, 3).reshape(-1, 8, 128)


def from_tiles(value, height, width):
    return value.reshape(height // 8, width // 128, 8, 128).transpose(0, 2, 1, 3).reshape(height, width)


def shards(cstates, drift, diffusivity, coarse_rate):
    cells = cstates[0]
    height, width = cells.shape
    parts = [to_tiles(cells), to_tiles(drift.reshape(-1, width)), to_tiles(diffusivity)]
    message = jnp.concatenate(parts)
    strips = lax.axis_size("space")
    inner = lax.ppermute(message, "space", [(i, i ^ 1) for i in range(strips)])
    outer = lax.ppermute(jnp.concatenate(parts + [jnp.zeros((1, 8, 128), jnp.float32)]), "space", [(i, (((i + 1) ^ 1) - 1) % strips) for i in range(strips)])
    parity = (lax.axis_index("space") % 2).reshape(1)
    history, first_half = near(parity, message, inner)
    second, first, term = far(parity, message, coarse_rate, outer, history, first_half)
    count = lax.axis_size("tm")
    ring = [[(k + FIRST) % count for k in range(count)]]
    place = (lax.axis_index("tm") + count - FIRST) % count
    rate = lax.dynamic_index_in_dim(to_tiles(coarse_rate), place, 0, keepdims=False)
    terms = lax.all_to_all(term, "tm", 0, 0, tiled=True, axis_index_groups=ring)
    second = passed_along(second, "tm", 2)
    first = passed_along(first, "tm", 1)
    points = coarse_solve(terms, rate)
    points = lax.all_to_all(points, "tm", 0, 0, tiled=True, axis_index_groups=ring)
    residual = second - first
    cpoints = from_tiles(points, height, width)
    return cpoints[None], residual[None]


def solution(mesh):
    placed = (P("tm", "space", None), P(None, "space", None), P("space", None), P("space", None))
    return jax.shard_map(
        shards,
        mesh=mesh,
        in_specs=placed,
        out_specs=(P("tm", "space", None), P("tm", "space", None)),
        check_vma=False,
    )
```

```python
import jax
import jax.numpy as jnp
from jax import lax
from jax.experimental import pallas as pl
from jax.experimental.pallas import tpu as pltpu
from jax.sharding import PartitionSpec as P

M = 8
FIRST = 11
nonlinear_weight = 0.05


def store_kernel(value, out, sem):
    copy = pltpu.make_async_copy(value, out, sem)
    copy.start()
    copy.wait()


def store(value):
    return pl.pallas_call(
        store_kernel,
        out_shape=jax.ShapeDtypeStruct(value.shape, jnp.float32),
        in_specs=[pl.BlockSpec(memory_space=pltpu.VMEM)],
        out_specs=pl.BlockSpec(memory_space=pl.ANY),
        scratch_shapes=[pltpu.SemaphoreType.DMA],
        compiler_params=pltpu.CompilerParams(vmem_limit_bytes=2 * 1024 * 1024),
        name="store",
    )(value)


def next_cell(u, above, below, right, left, coefs):
    spread = coefs[2] * ((above + below) + (right + left))
    along = (coefs[0] + (0.5 * nonlinear_weight) * u) * (right - left)
    across = coefs[1] * (above - below)
    return ((coefs[3] * u + spread) - along) - across


def load_state(strips, rows):
    tiles = rows.shape[0]
    for c in range(tiles):
        for k, strip in enumerate(strips):
            for r in range(2):
                rows[c, k * 16 + r * 8 : k * 16 + r * 8 + 8] = strip[r * tiles + c]


def load_coefs(strips, coef_rows):
    tiles = coef_rows.shape[1]
    for c in range(tiles):
        for k, strip in enumerate(strips):
            for r in range(2):
                place = slice(k * 16 + r * 8, k * 16 + r * 8 + 8)
                parts = [strip[(2 * f + r) * tiles + c] for f in (1, 2, 3)]
                coef_rows[0, c, place] = 0.5 * parts[0]
                coef_rows[1, c, place] = 0.5 * parts[1]
                coef_rows[2, c, place] = parts[2]
                coef_rows[3, c, place] = 1.0 - 4.0 * parts[2]


def near_kernel(parity, own, inner, history, first_half, rows, coef_rows, state, other, coefs):
    tiles, blocks = state.shape[0], state.shape[1]
    lane = lax.broadcasted_iota(jnp.int32, (8, 128), 1)
    is_last, is_first = lane == 127, lane == 0

    def one(src, dst):
        for i in range(blocks):
            to_left = lambda c: pltpu.roll(src[c % tiles, i], 127, 1)
            to_right = lambda c: pltpu.roll(src[c % tiles, i], 1, 1)
            ahead, behind, here = to_left(0), to_right(-1), to_right(0)
            for c in range(tiles):
                u = src[c, i]
                above = src[c, i + 1] if i + 1 < blocks else pltpu.roll(src[c, 0], 7, 0)
                below = src[c, i - 1] if i > 0 else pltpu.roll(src[c, blocks - 1], 1, 0)
                following = to_left(c + 1)
                right = jnp.where(is_last, following, ahead)
                left = jnp.where(is_first, behind, here)
                ahead, behind, here = following, here, to_right(c + 1)
                dst[c, i] = next_cell(u, above, below, right, left, [coefs[f, c, i] for f in range(4)])

    def run(strips, inner_is_after):
        load_coefs(strips, coef_rows)
        load_state(strips, rows)
        for c in range(tiles):
            for i in range(blocks):
                place = pl.ds(i, 8, stride=blocks)
                state[c, i] = rows[c, place, :]
                for f in range(4):
                    coefs[f, c, i] = coef_rows[f, c, place, :]

        def group(g, carry):
            for j in range(blocks):
                src, dst = (state, other) if j % 2 == 0 else (other, state)
                for w in range(2):
                    sub, block = divmod(j + w, blocks)
                    if inner_is_after:
                        row = (block, g + sub)
                    else:
                        row = (blocks - 1 - block, 7 - g - sub)
                    for c in range(tiles):
                        history[blocks * g + j, w, c : c + 1] = src[c, row[0], pl.ds(row[1], 1), :]
                one(src, dst)

            @pl.when(g == M // blocks - 1)
            def _():
                for c in range(tiles):
                    for i in range(blocks):
                        rows[c, pl.ds(i, 8, stride=blocks), :] = state[c, i]
                start = M if inner_is_after else 2 * M
                for c in range(tiles):
                    first_half[:, c * 128 : c * 128 + 128] = rows[c, start : start + M]

            return carry

        lax.fori_loop(0, 2 * M // blocks, group, 0)

    @pl.when(parity[0] == 0)
    def _():
        run((own, inner), True)

    @pl.when(parity[0] == 1)
    def _():
        run((inner, own), False)


def near(parity, own, inner):
    height, tiles = 16, own.shape[0] // 8
    width = tiles * 128
    return pl.pallas_call(
        near_kernel,
        out_shape=(
            jax.ShapeDtypeStruct((2 * M, 2, tiles, 128), jnp.float32),
            jax.ShapeDtypeStruct((M, width), jnp.float32),
        ),
        scratch_shapes=[
            pltpu.VMEM((tiles, 2 * height + 8, 128), jnp.float32),
            pltpu.VMEM((4, tiles, 2 * height + 8, 128), jnp.float32),
            pltpu.VMEM((tiles, 4, 8, 128), jnp.float32),
            pltpu.VMEM((tiles, 4, 8, 128), jnp.float32),
            pltpu.VMEM((4, tiles, 4, 8, 128), jnp.float32),
        ],
        in_specs=[pl.BlockSpec(memory_space=pltpu.SMEM)] + [pl.BlockSpec(memory_space=pltpu.VMEM)] * 2,
        compiler_params=pltpu.CompilerParams(vmem_limit_bytes=16 * 1024 * 1024),
        cost_estimate=pl.CostEstimate(flops=0, bytes_accessed=0, transcendentals=0),
        name="near",
    )(parity, own, inner)


def far_kernel(
    parity, own, rate, outer, history, first_half, second_out, first_out, term_out, rows, coef_rows, state, other
):
    tiles = state.shape[0]
    lane = lax.broadcasted_iota(jnp.int32, (8, 128), 1)
    is_last, is_first = lane == 127, lane == 0
    sub = lax.broadcasted_iota(jnp.int32, (8, 128), 0)

    def one(k, src, dst, outer_is_before):
        def column(c):
            c = c % tiles
            even, odd = src[c, 0], src[c, 1]
            joins = [jnp.broadcast_to(history[k, w, c : c + 1], (8, 128)) for w in range(2)]
            if outer_is_before:
                even_on = jnp.where(sub == 7, joins[0], pltpu.roll(even, 7, 0))
                odd_on = jnp.where(sub == 7, joins[1], pltpu.roll(odd, 7, 0))
                cells = [(odd, even_on, even), (even_on, odd_on, odd)]
            else:
                even_on = jnp.where(sub == 0, joins[1], pltpu.roll(even, 1, 0))
                odd_on = jnp.where(sub == 0, joins[0], pltpu.roll(odd, 1, 0))
                cells = [(odd_on, even, even_on), (even, odd, odd_on)]
            return cells, [pltpu.roll(u, 127, 1) for u, _, _ in cells], [pltpu.roll(u, 1, 1) for u, _, _ in cells]

        behind, here = column(-1), column(0)
        top = k + 1 if outer_is_before else 2 * M - 1 - k
        for c in range(tiles):
            ahead = column(c + 1)
            for i in range(2):
                u, above, below = here[0][i]
                right = jnp.where(is_last, ahead[1][i], here[1][i])
                left = jnp.where(is_first, behind[2][i], here[2][i])
                place = pl.ds(top + i, 8, stride=2)
                dst[c, i] = next_cell(u, above, below, right, left, [coef_rows[f, c, place, :] for f in range(4)])
            behind, here = here, ahead

    def unfold():
        for c in range(tiles):
            for i in range(2):
                rows[c, pl.ds(i, 8, stride=2), :] = state[c, i]

    def run(strips, outer_is_before):
        load_coefs(strips, coef_rows)
        load_state((outer,), rows)
        for c in range(tiles):
            for i in range(2):
                state[c, i] = rows[c, pl.ds(i, 8, stride=2), :]

        def pair(h, carry):
            @pl.when(h == M // 2)
            def _():
                unfold()
                for c in range(tiles):
                    cols = slice(c * 128, c * 128 + 128)
                    if outer_is_before:
                        first_out[0:M, cols] = rows[c, M : 2 * M]
                        first_out[M : 2 * M, cols] = first_half[:, cols]
                    else:
                        first_out[0:M, cols] = first_half[:, cols]
                        first_out[M : 2 * M, cols] = rows[c, 0:M]

            one(2 * h, state, other, outer_is_before)
            one(2 * h + 1, other, state, outer_is_before)
            return carry

        lax.fori_loop(0, M, pair, 0, unroll=True)

    @pl.when(parity[0] == 0)
    def _():
        run((outer, own), True)

    @pl.when(parity[0] == 1)
    def _():
        run((own, outer), False)

    unfold()
    for c in range(tiles):
        cols = slice(c * 128, c * 128 + 128)
        second_out[:, cols] = rows[c, 0 : 2 * M]
        for r in range(2):
            part = (slice(r * 8, r * 8 + 8), cols)
            term_out[r * tiles + c] = rows[c, r * 8 : r * 8 + 8] - jnp.exp(-rate[part]) * first_out[part]


def far(parity, own, rate, outer, history, first_half):
    height, width = rate.shape
    tiles = width // 128
    shape = lambda *s: jax.ShapeDtypeStruct(s, jnp.float32)
    return pl.pallas_call(
        far_kernel,
        out_shape=(shape(height, width), shape(height, width), shape(2 * tiles, 8, 128)),
        scratch_shapes=[
            pltpu.VMEM((tiles, height + 8, 128), jnp.float32),
            pltpu.VMEM((4, tiles, 2 * height + 8, 128), jnp.float32),
            pltpu.VMEM((tiles, 2, 8, 128), jnp.float32),
            pltpu.VMEM((tiles, 2, 8, 128), jnp.float32),
        ],
        in_specs=[pl.BlockSpec(memory_space=pltpu.SMEM)] + [pl.BlockSpec(memory_space=pltpu.VMEM)] * 5,
        compiler_params=pltpu.CompilerParams(vmem_limit_bytes=16 * 1024 * 1024),
        name="far",
    )(parity, own, rate, outer, history, first_half)


def solve_kernel(terms, rate, points):
    intervals, length = terms.shape[0], 8
    chains = intervals // length
    powers = [jnp.exp(-rate[...])]
    for _ in range(length - 1):
        powers.append(powers[-1] * powers[0])
    sums = [[terms[c * length]] for c in range(chains)]
    for k in range(1, length):
        for c in range(chains):
            sums[c].append(powers[0] * sums[c][-1] + terms[c * length + k])
    jump = powers[-1]
    closing, whole = sums[0][-1], jump
    for c in range(1, chains):
        closing = jump * closing + sums[c][-1]
        whole = whole * jump
    carry = closing / (1.0 - whole)
    for c in range(chains):
        for k in range(length):
            points[(c * length + k + 2) % intervals] = powers[k] * carry + sums[c][k]
        carry = jump * carry + sums[c][-1]


def coarse_solve(terms, rate):
    return pl.pallas_call(
        solve_kernel,
        out_shape=jax.ShapeDtypeStruct(terms.shape, jnp.float32),
        compiler_params=pltpu.CompilerParams(vmem_limit_bytes=2 * 1024 * 1024),
        name="coarse_solve",
    )(terms, rate)


def passed_along(value, axis, steps):
    count = lax.axis_size(axis)
    return lax.ppermute(value, axis, [(i, (i + steps) % count) for i in range(count)])


def to_tiles(value):
    height, width = value.shape
    return value.reshape(height // 8, 8, width // 128, 128).transpose(0, 2, 1, 3).reshape(-1, 8, 128)


def from_tiles(value, height, width):
    return value.reshape(height // 8, width // 128, 8, 128).transpose(0, 2, 1, 3).reshape(height, width)


def shards(cstates, drift, diffusivity, coarse_rate):
    cells = cstates[0]
    height, width = cells.shape
    parts = [to_tiles(cells), to_tiles(drift.reshape(-1, width)), to_tiles(diffusivity)]
    message = jnp.concatenate(parts)
    strips = lax.axis_size("space")
    inner = lax.ppermute(message, "space", [(i, i ^ 1) for i in range(strips)])
    outer = lax.ppermute(jnp.concatenate(parts + [jnp.zeros((1, 8, 128), jnp.float32)]), "space", [(i, (((i + 1) ^ 1) - 1) % strips) for i in range(strips)])
    parity = (lax.axis_index("space") % 2).reshape(1)
    history, first_half = near(parity, message, inner)
    second, first, term = far(parity, message, coarse_rate, outer, history, first_half)
    count = lax.axis_size("tm")
    ring = [[(k + FIRST) % count for k in range(count)]]
    place = (lax.axis_index("tm") + count - FIRST) % count
    rate = lax.dynamic_index_in_dim(to_tiles(coarse_rate), place, 0, keepdims=False)
    terms = lax.all_to_all(term, "tm", 0, 0, tiled=True, axis_index_groups=ring)
    second = passed_along(second, "tm", 2)
    first = passed_along(first, "tm", 1)
    points = coarse_solve(terms, rate)
    points = lax.all_to_all(points, "tm", 0, 0, tiled=True, axis_index_groups=ring)
    residual = second - first
    cpoints = from_tiles(points, height, width)
    return cpoints[None], residual[None]


def solution(mesh):
    placed = (P("tm", "space", None), P(None, "space", None), P("space", None), P("space", None))
    return jax.shard_map(
        shards,
        mesh=mesh,
        in_specs=placed,
        out_specs=(P("tm", "space", None), P("tm", "space", None)),
        check_vma=False,
    )
```
